32 devices in a mesh: grp: 4 (over z), box: 8 (over y, x, core).
Axes of the slice: x: 2, y: 2, z: 4, core: 2. Of those that a mesh axis runs over, the one named last changes fastest.
Arguments:
- weights: bfloat16 [4096, 8192], P(('grp', 'box')), may hold values from -6 to 6
- tables: bfloat16 [32, 2, 64, 64], replicated, may hold values from -0.5 to 0.5
- pattern: int32 [4096, 4], P(('grp', 'box')), may hold values from 0 to 31
- partner_slot: int32 [4096, 4], P(('grp', 'box')), may hold values from 0 to 127, as said below
- target_order: int32 [32, 128], P(('grp', 'box')), may hold values from 0 to 127, each once within a row
Outputs:
- targets: bfloat16 [4096, 8192], P(('grp', 'box'))
The draws below stay inside these ranges and needn't reach their ends.
Inputs may be any that keep to these rules, and one draw needn't show every extreme that they name: For each device and level, partner_slot over that device's boxes is a permutation of its positions; at the last level, 3, partner_slot[n, l] lies in the same block of 128 // 4 positions as n's own position.
All inputs are finite; a program needn't handle non-finite values.
Results may differ from the reference program's by a relative error of at most 0.0064.
Values may be sent and summed in bfloat16 or wider, within the bound.
A program may use at most 64 MiB of HBM per device.

```python
import jax
import jax.numpy as jnp
from jax import lax

R = 64
NRHS = 128
BPD = 128
NT = 32
LEVELS = 4
BOXES = 4096
N_GRP = 4
N_BOX = 8


def draw_partner_slot(key, part):
    key = jax.random.fold_in(key, 7)
    key_full = jax.random.fold_in(key, 1)
    key_block = jax.random.fold_in(key, 2)
    piece = BPD // N_GRP
    device_count = N_GRP * N_BOX
    full_scores = jax.random.randint(key_full, (device_count, LEVELS - 1, BPD), 0, 2 ** 18)
    full_scores = full_scores * BPD + jnp.arange(BPD, dtype=jnp.int32)
    full_order = jnp.argsort(full_scores, axis=-1, stable=True).astype(jnp.int32)
    scores = jax.random.randint(key_block, (device_count, 1, N_GRP, piece), 0, 2 ** 18)
    scores = scores * piece + jnp.arange(piece, dtype=jnp.int32)
    order = jnp.argsort(scores, axis=-1, stable=True).astype(jnp.int32)
    block_slots = order + (jnp.arange(N_GRP, dtype=jnp.int32) * piece)[:, None]
    block_slots = block_slots.reshape(device_count, 1, BPD)
    slots = jnp.concatenate([full_order, block_slots], axis=1)
    slots = jnp.transpose(slots, (0, 2, 1))
    return slots.reshape(device_count * BPD, LEVELS).astype(jnp.int32)


def set_ends(array, own_key, smallest, high):
    longest = array.shape.index(max(array.shape))
    spots = []
    for shift in (0, 1):
        where = [jax.random.randint(jax.random.fold_in(own_key, axis), (), 0, length) for axis, length in enumerate(array.shape)]
        where[longest] = (where[longest] + shift) % array.shape[longest]
        spots.append(tuple(where))
    return array.at[spots[0]].set(smallest).at[spots[1]].set(high)


def shard_levels(rng, extent, split, smallest, high):
    factor_of = 1.0
    for position, blocks in split:
        heights = jax.random.uniform(jax.random.fold_in(jax.random.fold_in(rng, 6), position), (blocks,), jnp.float32, smallest / len(split), high / len(split))
        factor_of = factor_of * jnp.repeat(jnp.exp(heights), extent[position] // blocks).reshape((-1,) + (1,) * (len(extent) - 1 - position))
    return factor_of


def gaussian(own_key, shape, spread, reach, pieces=(), kind=jnp.bfloat16):
    result = spread * jax.random.normal(own_key, shape, jnp.float32)
    if pieces:
        result = result * shard_levels(own_key, shape, pieces, -0.22, 0.18)
    return jnp.clip(result, -reach, reach).astype(kind)


def setup_inputs(seed: int = 0) -> dict:
    key_of = jax.random.split(jax.random.key(seed), 6)
    return {
        "weights": gaussian(key_of[0], (BOXES, R * NRHS), 1.0, 6.0, ((0, 32),)),
        "tables": gaussian(key_of[1], (NT, 2, R, R), (2 * R) ** -0.5, 0.5),
        "pattern": set_ends(jax.random.randint(key_of[2], (BOXES, LEVELS), 0, NT), jax.random.fold_in(key_of[2], 1), 0, NT - 1).astype(jnp.int32),
        "partner_slot": draw_partner_slot(jax.random.fold_in(key_of[5], 71), 0),
        "target_order": jax.vmap(lambda own: jax.random.permutation(own, BPD))(jax.random.split(key_of[4], (N_GRP * N_BOX))).reshape((N_GRP * N_BOX, BPD)).astype(jnp.int32),
    }


def reference(weights, tables, pattern, partner_slot, target_order):
    device_count = N_GRP * N_BOX
    box_bits = N_BOX.bit_length() - 1
    current = weights.reshape(device_count, BPD, R, NRHS)
    codes = pattern.reshape(device_count, BPD, LEVELS)
    slots = partner_slot.reshape(device_count, BPD, LEVELS)
    tables_wide = tables.astype(jnp.float32)
    for level_index in range(LEVELS):
        flip = 1 << (box_bits - 3 + level_index)

        def one_device(device):
            partner_dev = jnp.bitwise_xor(device, flip)
            mine = current[device].astype(jnp.float32)
            partner_rows = current[partner_dev][slots[device, :, level_index]].astype(jnp.float32)
            blocks = tables_wide[codes[device, :, level_index]]
            kept = jnp.einsum('jab,jbc->jac', blocks[:, 0], mine)
            moved = jnp.einsum('jab,jbc->jac', blocks[:, 1], partner_rows)
            return (kept + moved).astype(jnp.bfloat16)

        current = lax.map(one_device, jnp.arange(device_count, dtype=jnp.int32))
    piece = BPD // N_GRP
    grouped = current.reshape(N_GRP, N_BOX, N_GRP, piece, R, NRHS)
    grouped = jnp.transpose(grouped, (2, 1, 0, 3, 4, 5)).reshape(device_count, BPD, R, NRHS)
    picked = jnp.take_along_axis(grouped, target_order[:, :, None, None], axis=1)
    return picked.reshape(device_count * BPD, R * NRHS)
```

```python
import functools

import jax
import jax.numpy as jnp
from jax import lax
from jax.experimental import pallas as pl
from jax.experimental.pallas import tpu as pltpu
from jax.sharding import PartitionSpec as P

MESH = pl.DeviceIdType.MESH
COLS = 16
UNROLL = 4


def pick(ref, code_a, code_b, low_lanes):
    a = ref[code_a // 2]
    b = ref[code_b // 2]
    a = jnp.where(code_a % 2 == 1, pltpu.roll(a, 64, 1), a)
    b = jnp.where(code_b % 2 == 1, b, pltpu.roll(b, 64, 1))
    return jnp.where(low_lanes, a, b)


def kernel(groups, boxes, chunks, pairs, x_ref, tbl_ref, pat_ref, slot_ref, order_ref, meta_ref, out_ref, *scratch):
    it = iter(scratch)
    recv = [[next(it) for _ in range(chunks)] for _ in range(3)]
    made = [[next(it) for _ in range(chunks)] for _ in range(3)]
    zbuf = [next(it) for _ in range(chunks)]
    meta_recv, meta_smem, par_s, pat_s = (next(it) for _ in range(4))
    send_sem, recv_sem, zsend_sem, zrecv_sem, zown_sem, msend_sem, mrecv_sem, mown_sem = it

    n_box = 2 * pairs
    piece = n_box // groups
    ppiece = pairs // groups
    grp = lax.axis_index("grp")
    box = lax.axis_index("box")
    box_bits = boxes.bit_length() - 1
    partners = []
    for level in range(3):
        flip = 1 << (box_bits - 3 + level)
        bit = (box // flip) % 2
        partners.append(box + flip - 2 * flip * bit)

    barrier = pltpu.get_barrier_semaphore()
    for other in partners:
        pl.semaphore_signal(barrier, inc=1, device_id={"box": other}, device_id_type=MESH)
    for off in range(1, groups):
        pl.semaphore_signal(barrier, inc=1, device_id={"grp": (grp + off) % groups}, device_id_type=MESH)
    pl.semaphore_wait(barrier, 3 + groups - 1)

    def level_copy(level, c):
        src = x_ref.at[c] if level == 0 else made[level - 1][c]
        return pltpu.make_async_remote_copy(
            src_ref=src,
            dst_ref=recv[level][c],
            send_sem=send_sem.at[level, c],
            recv_sem=recv_sem.at[level, c],
            device_id={"box": partners[level]},
            device_id_type=MESH,
        )

    def z_copy(c, off):
        to = (grp + off) % groups
        return pltpu.make_async_remote_copy(
            src_ref=made[2][c].at[pl.ds(to * ppiece, ppiece)],
            dst_ref=zbuf[c].at[pl.ds(grp * ppiece, ppiece)],
            send_sem=zsend_sem.at[c, off - 1],
            recv_sem=zrecv_sem.at[c, off - 1],
            device_id={"grp": to},
            device_id_type=MESH,
        )

    def z_own(c):
        mine = pl.ds(grp * ppiece, ppiece)
        return pltpu.make_async_copy(made[2][c].at[mine], zbuf[c].at[mine], zown_sem.at[c])

    def meta_copy(off):
        to = (grp + off) % groups
        return pltpu.make_async_remote_copy(
            src_ref=meta_ref.at[to],
            dst_ref=meta_recv.at[grp],
            send_sem=msend_sem.at[off - 1],
            recv_sem=mrecv_sem.at[off - 1],
            device_id={"grp": to},
            device_id_type=MESH,
        )

    for c in range(chunks):
        level_copy(0, c).start()
    for off in range(1, groups):
        meta_copy(off).start()
    pltpu.make_async_copy(meta_ref.at[grp], meta_recv.at[grp], mown_sem.at[0]).start()

    low_lanes = lax.broadcasted_iota(jnp.int32, (COLS, 128), 1) < 64

    def combine(own, other, pa, pb):
        left = jnp.concatenate([own, other], axis=1)
        right = jnp.concatenate(
            [tbl_ref[0, pa, 0], tbl_ref[1, pb, 0], tbl_ref[0, pa, 1], tbl_ref[1, pb, 1]], axis=0
        )
        return jnp.dot(left, right, preferred_element_type=jnp.float32).astype(jnp.bfloat16)

    def compute(level, c):
        level_copy(level, c).wait_recv()
        src = x_ref.at[c] if level == 0 else made[level - 1][c]

        @pl.loop(0, pairs // UNROLL)
        def _(i):
            for u in range(UNROLL):
                j = i * UNROLL + u
                at = level * n_box + 2 * j
                other = pick(recv[level][c], slot_ref[at], slot_ref[at + 1], low_lanes)
                made[level][c][j] = combine(src[j], other, pat_ref[at], pat_ref[at + 1])

        if level < 2:
            level_copy(level + 1, c).start()
        else:
            for off in range(1, groups):
                z_copy(c, off).start()
            z_own(c).start()

    def prepare_last():
        for off in range(1, groups):
            meta_copy(off).wait_recv()
        pltpu.make_async_copy(meta_ref.at[grp], meta_recv.at[grp], mown_sem.at[0]).wait()
        copy = pltpu.make_async_copy(meta_recv, meta_smem, mown_sem.at[1])
        copy.start()
        copy.wait()

        @pl.loop(0, n_box)
        def _(q):
            z = order_ref[q]
            h = z // piece
            s = z % piece
            par_s[q] = (h + 1 - 2 * (h % 2)) * piece + meta_smem[h, 1, s]
            pat_s[q] = meta_smem[h, 0, s]

    def last(c):
        for off in range(1, groups):
            z_copy(c, off).wait_recv()
        z_own(c).wait()

        @pl.loop(0, pairs // UNROLL)
        def _(i):
            for u in range(UNROLL):
                j = i * UNROLL + u
                own = pick(zbuf[c], order_ref[2 * j], order_ref[2 * j + 1], low_lanes)
                other = pick(zbuf[c], par_s[2 * j], par_s[2 * j + 1], low_lanes)
                out_ref[c, j] = combine(own, other, pat_s[2 * j], pat_s[2 * j + 1])

    for c in range(chunks):
        compute(0, c)
    prepare_last()
    for t in range(chunks + 2):
        for level in (1, 2, 3):
            c = t - (level - 1)
            if 0 <= c < chunks:
                if level < 3:
                    compute(level, c)
                else:
                    last(c)

    for c in range(chunks):
        for level in range(3):
            level_copy(level, c).wait_send()
        for off in range(1, groups):
            z_copy(c, off).wait_send()
    for off in range(1, groups):
        meta_copy(off).wait_send()


def body(weights, tables, pattern, partner_slot, target_order):
    n_box, width = weights.shape
    kinds, _, rank, _ = tables.shape
    nrhs = width // rank
    chunks = nrhs // COLS
    pairs = n_box // 2
    groups = lax.axis_size("grp")
    boxes = lax.axis_size("box")
    piece = n_box // groups

    with jax.named_scope("pack_weights"):
        x = weights.reshape(pairs, 2, rank, chunks, COLS)
        x = jnp.transpose(x, (3, 0, 4, 1, 2)).reshape(chunks, pairs, COLS, 2 * rank)
    with jax.named_scope("pack_tables"):
        turned = jnp.swapaxes(tables, 2, 3)
        zero = jnp.zeros_like(turned)
        tbl = jnp.stack([jnp.concatenate([turned, zero], 3), jnp.concatenate([zero, turned], 3)])
    pat = jnp.transpose(pattern[:, :3]).reshape(-1)
    slot = jnp.transpose(partner_slot[:, :3]).reshape(-1)
    meta = jnp.stack([pattern[:, 3].reshape(groups, piece), partner_slot[:, 3].reshape(groups, piece) % piece], 1)
    meta = jnp.pad(meta, ((0, 0), (0, 6), (0, 128 - piece)))

    block = (pairs, COLS, 2 * rank)
    vmem = pl.BlockSpec(memory_space=pltpu.VMEM)
    smem = pl.BlockSpec(memory_space=pltpu.SMEM)
    dma = pltpu.SemaphoreType.DMA
    out = pl.pallas_call(
        functools.partial(kernel, groups, boxes, chunks, pairs),
        out_shape=jax.ShapeDtypeStruct((chunks,) + block, jnp.bfloat16),
        in_specs=[vmem, vmem, smem, smem, smem, vmem],
        out_specs=vmem,
        scratch_shapes=[pltpu.VMEM(block, jnp.bfloat16)] * (7 * chunks)
        + [
            pltpu.VMEM((groups, 8, 128), jnp.int32),
            pltpu.SMEM((groups, 8, 128), jnp.int32),
            pltpu.SMEM((n_box,), jnp.int32),
            pltpu.SMEM((n_box,), jnp.int32),
            dma((3, chunks)),
            dma((3, chunks)),
            dma((chunks, groups - 1)),
            dma((chunks, groups - 1)),
            dma((chunks,)),
            dma((groups - 1,)),
            dma((groups - 1,)),
            dma((2,)),
        ],
        compiler_params=pltpu.CompilerParams(
            collective_id=0, has_side_effects=True, vmem_limit_bytes=40 * 1024 * 1024
        ),
        cost_estimate=pl.CostEstimate(flops=4 * 2 * n_box * rank * 2 * rank * nrhs, bytes_accessed=4 * n_box * width, transcendentals=0),
    )(x, tbl, pat, slot, target_order[0], meta)

    with jax.named_scope("unpack_targets"):
        out = out.reshape(chunks, pairs, COLS, 2, rank)
        return jnp.transpose(out, (1, 3, 4, 0, 2)).reshape(n_box, width)


def solution(mesh):
    placed = (
        P(("grp", "box"), None),
        P(),
        P(("grp", "box"), None),
        P(("grp", "box"), None),
        P(("grp", "box"), None),
    )
    return jax.shard_map(
        body, mesh=mesh, in_specs=placed, out_specs=P(("grp", "box"), None), check_vma=False
    )
```

```python
import functools

import jax
import jax.numpy as jnp
from jax import lax
from jax.experimental import pallas as pl
from jax.experimental.pallas import tpu as pltpu
from jax.sharding import PartitionSpec as P

MESH = pl.DeviceIdType.MESH
COLS = 16
UNROLL = 4


def pick(ref, code_a, code_b, low_lanes):
    a = ref[code_a // 2]
    b = ref[code_b // 2]
    a = jnp.where(code_a % 2 == 1, pltpu.roll(a, 64, 1), a)
    b = jnp.where(code_b % 2 == 1, b, pltpu.roll(b, 64, 1))
    return jnp.where(low_lanes, a, b)


def kernel(groups, boxes, chunks, pairs, x_ref, tbl_ref, pat_ref, slot_ref, order_ref, meta_ref, out_ref, *scratch):
    it = iter(scratch)
    recv = [[next(it) for _ in range(chunks)] for _ in range(3)]
    made = [[next(it) for _ in range(chunks)] for _ in range(3)]
    zbuf = [next(it) for _ in range(chunks)]
    meta_recv, meta_smem, par_s, pat_s = (next(it) for _ in range(4))
    send_sem, recv_sem, zsend_sem, zrecv_sem, zown_sem, msend_sem, mrecv_sem, mown_sem = it

    n_box = 2 * pairs
    piece = n_box // groups
    ppiece = pairs // groups
    grp = lax.axis_index("grp")
    box = lax.axis_index("box")
    box_bits = boxes.bit_length() - 1
    partners = []
    for level in range(3):
        flip = 1 << (box_bits - 3 + level)
        bit = (box // flip) % 2
        partners.append(box + flip - 2 * flip * bit)

    barrier = pltpu.get_barrier_semaphore()
    for other in partners:
        pl.semaphore_signal(barrier, inc=1, device_id={"box": other}, device_id_type=MESH)
    for off in range(1, groups):
        pl.semaphore_signal(barrier, inc=1, device_id={"grp": (grp + off) % groups}, device_id_type=MESH)
    pl.semaphore_wait(barrier, 3 + groups - 1)

    def level_copy(level, c):
        src = x_ref.at[c] if level == 0 else made[level - 1][c]
        return pltpu.make_async_remote_copy(
            src_ref=src,
            dst_ref=recv[level][c],
            send_sem=send_sem.at[level, c],
            recv_sem=recv_sem.at[level, c],
            device_id={"box": partners[level]},
            device_id_type=MESH,
        )

    def z_copy(c, off):
        to = (grp + off) % groups
        return pltpu.make_async_remote_copy(
            src_ref=made[2][c].at[pl.ds(to * ppiece, ppiece)],
            dst_ref=zbuf[c].at[pl.ds(grp * ppiece, ppiece)],
            send_sem=zsend_sem.at[c, off - 1],
            recv_sem=zrecv_sem.at[c, off - 1],
            device_id={"grp": to},
            device_id_type=MESH,
        )

    def z_own(c):
        mine = pl.ds(grp * ppiece, ppiece)
        return pltpu.make_async_copy(made[2][c].at[mine], zbuf[c].at[mine], zown_sem.at[c])

    def meta_copy(off):
        to = (grp + off) % groups
        return pltpu.make_async_remote_copy(
            src_ref=meta_ref.at[to],
            dst_ref=meta_recv.at[grp],
            send_sem=msend_sem.at[off - 1],
            recv_sem=mrecv_sem.at[off - 1],
            device_id={"grp": to},
            device_id_type=MESH,
        )

    for c in range(chunks):
        level_copy(0, c).start()
    for off in range(1, groups):
        meta_copy(off).start()
    pltpu.make_async_copy(meta_ref.at[grp], meta_recv.at[grp], mown_sem.at[0]).start()

    low_lanes = lax.broadcasted_iota(jnp.int32, (COLS, 128), 1) < 64

    def combine(own, other, pa, pb):
        left = jnp.concatenate([own, other], axis=1)
        right = jnp.concatenate(
            [tbl_ref[0, pa, 0], tbl_ref[1, pb, 0], tbl_ref[0, pa, 1], tbl_ref[1, pb, 1]], axis=0
        )
        return jnp.dot(left, right, preferred_element_type=jnp.float32).astype(jnp.bfloat16)

    def compute(level, c):
        level_copy(level, c).wait_recv()
        src = x_ref.at[c] if level == 0 else made[level - 1][c]

        @pl.loop(0, pairs // UNROLL)
        def _(i):
            for u in range(UNROLL):
                j = i * UNROLL + u
                at = level * n_box + 2 * j
                other = pick(recv[level][c], slot_ref[at], slot_ref[at + 1], low_lanes)
                made[level][c][j] = combine(src[j], other, pat_ref[at], pat_ref[at + 1])

        if level < 2:
            level_copy(level + 1, c).start()
        else:
            for off in range(1, groups):
                z_copy(c, off).start()
            z_own(c).start()

    def prepare_last():
        for off in range(1, groups):
            meta_copy(off).wait_recv()
        pltpu.make_async_copy(meta_ref.at[grp], meta_recv.at[grp], mown_sem.at[0]).wait()
        copy = pltpu.make_async_copy(meta_recv, meta_smem, mown_sem.at[1])
        copy.start()
        copy.wait()

        @pl.loop(0, n_box)
        def _(q):
            z = order_ref[q]
            h = z // piece
            s = z % piece
            par_s[q] = (h + 1 - 2 * (h % 2)) * piece + meta_smem[h, 1, s]
            pat_s[q] = meta_smem[h, 0, s]

    def last(c):
        for off in range(1, groups):
            z_copy(c, off).wait_recv()
        z_own(c).wait()

        @pl.loop(0, pairs // UNROLL)
        def _(i):
            for u in range(UNROLL):
                j = i * UNROLL + u
                own = pick(zbuf[c], order_ref[2 * j], order_ref[2 * j + 1], low_lanes)
                other = pick(zbuf[c], par_s[2 * j], par_s[2 * j + 1], low_lanes)
                out_ref[c, j] = combine(own, other, pat_s[2 * j], pat_s[2 * j + 1])

    for c in range(chunks):
        compute(0, c)
    prepare_last()
    for t in range(chunks + 2):
        for level in (1, 2, 3):
            c = t - (level - 1)
            if 0 <= c < chunks:
                if level < 3:
                    compute(level, c)
                else:
                    last(c)

    for c in range(chunks):
        for level in range(3):
            level_copy(level, c).wait_send()
        for off in range(1, groups):
            z_copy(c, off).wait_send()
    for off in range(1, groups):
        meta_copy(off).wait_send()


def pack_kernel(w_ref, x_ref):
    chunks = x_ref.shape[0]
    rank = w_ref.shape[1] // 128
    w = jnp.stack([w_ref[:, a * 128 : (a + 1) * 128].astype(jnp.float32) for a in range(rank)])
    w = jnp.transpose(w, (1, 0, 2))
    for i in range(w.shape[0] // 2):
        turned = jnp.transpose(w[2 * i : 2 * i + 2].reshape(2 * rank, 128))
        x_ref[:, i] = turned.astype(jnp.bfloat16).reshape(chunks, COLS, 2 * rank)


def unpack_kernel(y_ref, o_ref):
    rank = o_ref.shape[1] // 128
    boxes = []
    for i in range(y_ref.shape[1]):
        y = y_ref[:, i].reshape(128, 2 * rank).astype(jnp.float32)
        boxes.append(jnp.transpose(y).reshape(2, rank, 128))
    o = jnp.transpose(jnp.concatenate(boxes, axis=0), (1, 0, 2))
    for a in range(rank):
        o_ref[:, a * 128 : (a + 1) * 128] = o[a].astype(jnp.bfloat16)


def pack(w, rank):
    n_box, width = w.shape
    chunks = width // rank // COLS
    return pl.pallas_call(
        pack_kernel,
        out_shape=jax.ShapeDtypeStruct((chunks, n_box // 2, COLS, 2 * rank), w.dtype),
        grid=(n_box // 16,),
        in_specs=[pl.BlockSpec((16, width), lambda i: (i, 0))],
        out_specs=pl.BlockSpec((chunks, 8, COLS, 2 * rank), lambda i: (0, i, 0, 0)),
        compiler_params=pltpu.CompilerParams(vmem_limit_bytes=32 * 1024 * 1024),
    )(w)


def unpack(y, rank):
    chunks, pairs = y.shape[:2]
    width = rank * chunks * COLS
    return pl.pallas_call(
        unpack_kernel,
        out_shape=jax.ShapeDtypeStruct((2 * pairs, width), y.dtype),
        grid=(pairs // 8,),
        in_specs=[pl.BlockSpec((chunks, 8, COLS, 2 * rank), lambda i: (0, i, 0, 0))],
        out_specs=pl.BlockSpec((16, width), lambda i: (i, 0)),
        compiler_params=pltpu.CompilerParams(vmem_limit_bytes=32 * 1024 * 1024),
    )(y)


def body(weights, tables, pattern, partner_slot, target_order):
    n_box, width = weights.shape
    kinds, _, rank, _ = tables.shape
    nrhs = width // rank
    chunks = nrhs // COLS
    pairs = n_box // 2
    groups = lax.axis_size("grp")
    boxes = lax.axis_size("box")
    piece = n_box // groups

    with jax.named_scope("pack_weights"):
        x = pack(weights, rank)
    with jax.named_scope("pack_tables"):
        turned = jnp.swapaxes(tables, 2, 3)
        zero = jnp.zeros_like(turned)
        tbl = jnp.stack([jnp.concatenate([turned, zero], 3), jnp.concatenate([zero, turned], 3)])
    pat = jnp.transpose(pattern[:, :3]).reshape(-1)
    slot = jnp.transpose(partner_slot[:, :3]).reshape(-1)
    meta = jnp.stack([pattern[:, 3].reshape(groups, piece), partner_slot[:, 3].reshape(groups, piece) % piece], 1)
    meta = jnp.pad(meta, ((0, 0), (0, 6), (0, 128 - piece)))

    block = (pairs, COLS, 2 * rank)
    vmem = pl.BlockSpec(memory_space=pltpu.VMEM)
    smem = pl.BlockSpec(memory_space=pltpu.SMEM)
    dma = pltpu.SemaphoreType.DMA
    out = pl.pallas_call(
        functools.partial(kernel, groups, boxes, chunks, pairs),
        out_shape=jax.ShapeDtypeStruct((chunks,) + block, jnp.bfloat16),
        in_specs=[vmem, vmem, smem, smem, smem, vmem],
        out_specs=vmem,
        scratch_shapes=[pltpu.VMEM(block, jnp.bfloat16)] * (7 * chunks)
        + [
            pltpu.VMEM((groups, 8, 128), jnp.int32),
            pltpu.SMEM((groups, 8, 128), jnp.int32),
            pltpu.SMEM((n_box,), jnp.int32),
            pltpu.SMEM((n_box,), jnp.int32),
            dma((3, chunks)),
            dma((3, chunks)),
            dma((chunks, groups - 1)),
            dma((chunks, groups - 1)),
            dma((chunks,)),
            dma((groups - 1,)),
            dma((groups - 1,)),
            dma((2,)),
        ],
        compiler_params=pltpu.CompilerParams(
            collective_id=0, has_side_effects=True, vmem_limit_bytes=40 * 1024 * 1024
        ),
        cost_estimate=pl.CostEstimate(flops=4 * 2 * n_box * rank * 2 * rank * nrhs, bytes_accessed=4 * n_box * width, transcendentals=0),
    )(x, tbl, pat, slot, target_order[0], meta)

    with jax.named_scope("unpack_targets"):
        return unpack(out, rank)


def solution(mesh):
    placed = (
        P(("grp", "box"), None),
        P(),
        P(("grp", "box"), None),
        P(("grp", "box"), None),
        P(("grp", "box"), None),
    )
    return jax.shard_map(
        body, mesh=mesh, in_specs=placed, out_specs=P(("grp", "box"), None), check_vma=False
    )
```

```python
import functools

import jax
import jax.numpy as jnp
from jax import lax
from jax.experimental import pallas as pl
from jax.experimental.pallas import tpu as pltpu
from jax.sharding import PartitionSpec as P

MESH = pl.DeviceIdType.MESH
COLS = 16
UNROLL = 32


def pick(ref, code_low, code_high, low_lanes):
    a = ref[code_low >> 1]
    b = ref[code_high >> 1]
    a = pltpu.roll(a, (code_low & 1) * 64, 1)
    b = pltpu.roll(b, 64 - (code_high & 1) * 64, 1)
    return jnp.where(low_lanes, a, b)


def kernel(groups, boxes, chunks, pairs, x_ref, tbl_ref, pat_ref, slot_ref, order_ref, meta_ref, out_ref, *scratch):
    it = iter(scratch)
    recv = [[next(it) for _ in range(chunks)] for _ in range(3)]
    made = [[next(it) for _ in range(chunks)] for _ in range(3)]
    zbuf = [next(it) for _ in range(chunks)]
    meta_recv, meta_smem, par_s, pat_s = (next(it) for _ in range(4))
    send_sem, recv_sem, zsend_sem, zrecv_sem, zown_sem, msend_sem, mrecv_sem, mown_sem = it

    n_box = 2 * pairs
    piece = n_box // groups
    ppiece = pairs // groups
    grp = lax.axis_index("grp")
    box = lax.axis_index("box")
    box_bits = boxes.bit_length() - 1
    partners = []
    for level in range(3):
        flip = 1 << (box_bits - 3 + level)
        bit = (box // flip) % 2
        partners.append(box + flip - 2 * flip * bit)

    barrier = pltpu.get_barrier_semaphore()
    for other in partners:
        pl.semaphore_signal(barrier, inc=1, device_id={"box": other}, device_id_type=MESH)
    for off in range(1, groups):
        pl.semaphore_signal(barrier, inc=1, device_id={"grp": (grp + off) % groups}, device_id_type=MESH)
    pl.semaphore_wait(barrier, 3 + groups - 1)

    def level_copy(level, c):
        src = x_ref.at[c] if level == 0 else made[level - 1][c]
        return pltpu.make_async_remote_copy(
            src_ref=src,
            dst_ref=recv[level][c],
            send_sem=send_sem.at[level, c],
            recv_sem=recv_sem.at[level, c],
            device_id={"box": partners[level]},
            device_id_type=MESH,
        )

    def z_copy(c, off):
        to = (grp + off) % groups
        return pltpu.make_async_remote_copy(
            src_ref=made[2][c].at[pl.ds(to * ppiece, ppiece)],
            dst_ref=zbuf[c].at[pl.ds(grp * ppiece, ppiece)],
            send_sem=zsend_sem.at[c, off - 1],
            recv_sem=zrecv_sem.at[c, off - 1],
            device_id={"grp": to},
            device_id_type=MESH,
        )

    def z_own(c):
        mine = pl.ds(grp * ppiece, ppiece)
        return pltpu.make_async_copy(made[2][c].at[mine], zbuf[c].at[mine], zown_sem.at[c])

    def meta_copy(off):
        to = (grp + off) % groups
        return pltpu.make_async_remote_copy(
            src_ref=meta_ref.at[to],
            dst_ref=meta_recv.at[grp],
            send_sem=msend_sem.at[off - 1],
            recv_sem=mrecv_sem.at[off - 1],
            device_id={"grp": to},
            device_id_type=MESH,
        )

    for c in range(chunks):
        level_copy(0, c).start()
    for off in range(1, groups):
        meta_copy(off).start()
    pltpu.make_async_copy(meta_ref.at[grp], meta_recv.at[grp], mown_sem.at[0]).start()

    low_lanes = lax.broadcasted_iota(jnp.int32, (COLS, 128), 1) < 64

    low_table = lax.broadcasted_iota(jnp.int32, (128, 128), 1) < 64

    def combine(own, other, pa, pb):
        left = jnp.concatenate([jnp.where(low_lanes, own, other), jnp.where(low_lanes, other, own)], axis=0)
        right = jnp.where(low_table, tbl_ref[pa], tbl_ref[pb])
        both = jnp.dot(left, right, preferred_element_type=jnp.float32)
        return jnp.where(low_lanes, both[:COLS], both[COLS:]).astype(jnp.bfloat16)

    def compute(level, c):
        level_copy(level, c).wait_recv()
        src = x_ref.at[c] if level == 0 else made[level - 1][c]

        @pl.loop(0, pairs // UNROLL)
        def _(i):
            done = []
            for u in range(UNROLL):
                j = i * UNROLL + u
                at = level * n_box + 2 * j
                other = pick(recv[level][c], slot_ref[at + 1], slot_ref[at], low_lanes)
                done.append(combine(src[j], other, pat_ref[at], pat_ref[at + 1]))
            for u in range(UNROLL):
                made[level][c][i * UNROLL + u] = done[u]

        if level < 2:
            level_copy(level + 1, c).start()
        else:
            for off in range(1, groups):
                z_copy(c, off).start()
            z_own(c).start()

    def prepare_last():
        for off in range(1, groups):
            meta_copy(off).wait_recv()
        pltpu.make_async_copy(meta_ref.at[grp], meta_recv.at[grp], mown_sem.at[0]).wait()
        copy = pltpu.make_async_copy(meta_recv, meta_smem, mown_sem.at[1])
        copy.start()
        copy.wait()

        @pl.loop(0, n_box)
        def _(q):
            z = order_ref[q]
            h = z // piece
            s = z % piece
            par_s[q] = (h + 1 - 2 * (h % 2)) * piece + meta_smem[h, 1, s]
            pat_s[q] = meta_smem[h, 0, s]

    def last(c):
        for off in range(1, groups):
            z_copy(c, off).wait_recv()
        z_own(c).wait()

        @pl.loop(0, pairs // UNROLL)
        def _(i):
            done = []
            for u in range(UNROLL):
                j = i * UNROLL + u
                own = pick(zbuf[c], order_ref[2 * j], order_ref[2 * j + 1], low_lanes)
                other = pick(zbuf[c], par_s[2 * j + 1], par_s[2 * j], low_lanes)
                done.append(combine(own, other, pat_s[2 * j], pat_s[2 * j + 1]))
            for u in range(UNROLL):
                out_ref[c, i * UNROLL + u] = done[u]

    for c in range(chunks):
        compute(0, c)
    prepare_last()
    for t in range(chunks + 2):
        for level in (1, 2, 3):
            c = t - (level - 1)
            if 0 <= c < chunks:
                if level < 3:
                    compute(level, c)
                else:
                    last(c)

    for c in range(chunks):
        for level in range(3):
            level_copy(level, c).wait_send()
        for off in range(1, groups):
            z_copy(c, off).wait_send()
    for off in range(1, groups):
        meta_copy(off).wait_send()


def pack_kernel(w_ref, x_ref):
    chunks = x_ref.shape[0]
    rank = w_ref.shape[1] // 128
    w = jnp.stack([w_ref[:, a * 128 : (a + 1) * 128].astype(jnp.float32) for a in range(rank)])
    w = jnp.transpose(w, (1, 0, 2))
    for i in range(w.shape[0] // 2):
        turned = jnp.transpose(w[2 * i : 2 * i + 2].reshape(2 * rank, 128))
        x_ref[:, i] = turned.astype(jnp.bfloat16).reshape(chunks, COLS, 2 * rank)


def unpack_kernel(y_ref, o_ref):
    rank = o_ref.shape[1] // 128
    boxes = []
    for i in range(y_ref.shape[1]):
        y = y_ref[:, i].reshape(128, 2 * rank).astype(jnp.float32)
        boxes.append(jnp.transpose(y).reshape(2, rank, 128))
    o = jnp.transpose(jnp.concatenate(boxes, axis=0), (1, 0, 2))
    for a in range(rank):
        o_ref[:, a * 128 : (a + 1) * 128] = o[a].astype(jnp.bfloat16)


def pack(w, rank):
    n_box, width = w.shape
    chunks = width // rank // COLS
    return pl.pallas_call(
        pack_kernel,
        out_shape=jax.ShapeDtypeStruct((chunks, n_box // 2, COLS, 2 * rank), w.dtype),
        grid=(n_box // 16,),
        in_specs=[pl.BlockSpec((16, width), lambda i: (i, 0))],
        out_specs=pl.BlockSpec((chunks, 8, COLS, 2 * rank), lambda i: (0, i, 0, 0)),
        compiler_params=pltpu.CompilerParams(vmem_limit_bytes=32 * 1024 * 1024),
    )(w)


def unpack(y, rank):
    chunks, pairs = y.shape[:2]
    width = rank * chunks * COLS
    return pl.pallas_call(
        unpack_kernel,
        out_shape=jax.ShapeDtypeStruct((2 * pairs, width), y.dtype),
        grid=(pairs // 8,),
        in_specs=[pl.BlockSpec((chunks, 8, COLS, 2 * rank), lambda i: (0, i, 0, 0))],
        out_specs=pl.BlockSpec((16, width), lambda i: (i, 0)),
        compiler_params=pltpu.CompilerParams(vmem_limit_bytes=32 * 1024 * 1024),
    )(y)


def body(weights, tables, pattern, partner_slot, target_order):
    n_box, width = weights.shape
    kinds, _, rank, _ = tables.shape
    nrhs = width // rank
    chunks = nrhs // COLS
    pairs = n_box // 2
    groups = lax.axis_size("grp")
    boxes = lax.axis_size("box")
    piece = n_box // groups

    with jax.named_scope("pack_weights"):
        x = pack(weights, rank)
    with jax.named_scope("pack_tables"):
        turned = jnp.swapaxes(tables, 2, 3)
        first, second = turned[:, 0], turned[:, 1]
        tbl = jnp.concatenate([jnp.concatenate([first, second], 1), jnp.concatenate([second, first], 1)], 2)
    pat = jnp.transpose(pattern[:, :3]).reshape(-1)
    slot = jnp.transpose(partner_slot[:, :3]).reshape(-1)
    meta = jnp.stack([pattern[:, 3].reshape(groups, piece), partner_slot[:, 3].reshape(groups, piece) % piece], 1)
    meta = jnp.pad(meta, ((0, 0), (0, 6), (0, 128 - piece)))

    block = (pairs, COLS, 2 * rank)
    vmem = pl.BlockSpec(memory_space=pltpu.VMEM)
    smem = pl.BlockSpec(memory_space=pltpu.SMEM)
    dma = pltpu.SemaphoreType.DMA
    out = pl.pallas_call(
        functools.partial(kernel, groups, boxes, chunks, pairs),
        out_shape=jax.ShapeDtypeStruct((chunks,) + block, jnp.bfloat16),
        in_specs=[vmem, vmem, smem, smem, smem, vmem],
        out_specs=vmem,
        scratch_shapes=[pltpu.VMEM(block, jnp.bfloat16)] * (7 * chunks)
        + [
            pltpu.VMEM((groups, 8, 128), jnp.int32),
            pltpu.SMEM((groups, 8, 128), jnp.int32),
            pltpu.SMEM((n_box,), jnp.int32),
            pltpu.SMEM((n_box,), jnp.int32),
            dma((3, chunks)),
            dma((3, chunks)),
            dma((chunks, groups - 1)),
            dma((chunks, groups - 1)),
            dma((chunks,)),
            dma((groups - 1,)),
            dma((groups - 1,)),
            dma((2,)),
        ],
        compiler_params=pltpu.CompilerParams(
            collective_id=0, has_side_effects=True, vmem_limit_bytes=40 * 1024 * 1024
        ),
        cost_estimate=pl.CostEstimate(flops=4 * 2 * n_box * rank * 2 * rank * nrhs, bytes_accessed=4 * n_box * width, transcendentals=0),
    )(x, tbl, pat, slot, target_order[0], meta)

    with jax.named_scope("unpack_targets"):
        return unpack(out, rank)


def solution(mesh):
    placed = (
        P(("grp", "box"), None),
        P(),
        P(("grp", "box"), None),
        P(("grp", "box"), None),
        P(("grp", "box"), None),
    )
    return jax.shard_map(
        body, mesh=mesh, in_specs=placed, out_specs=P(("grp", "box"), None), check_vma=False
    )
```
